512 devices in a mesh: row: 4 (over y_hi), col: 16 (over x, y_lo, core), layer: 8 (over z).
Axes of the slice: x: 4, y: 8 (y_hi: 4, y_lo: 2; y = y_hi * 2 + y_lo), z: 8, core: 2. Of those that a mesh axis runs over, the one named last changes fastest.
Arguments:
- density: float32 [4096, 4096], P(('row', 'layer'), 'col'), as said below
- pattern: int32 [32, 32], replicated, may hold values from 0 to 1, as said below
Outputs:
- square: float32 [4096, 4096], P(('row', 'layer'), 'col')
- purified: float32 [4096, 4096], P(('row', 'layer'), 'col')
The draws below stay inside these ranges and needn't reach their ends.
Inputs may be any that keep to these rules, and one draw needn't show every extreme that they name: pattern is symmetric, holds only 0 and 1, and its diagonal is 1. density is symmetric.
All inputs are finite; a program needn't handle non-finite values.
Results may differ from the reference program's by a relative error of at most 0.0001.
Values sent between devices are 32-bit elements; how exact they have to be, the bound alone decides.
No kernel may reach another device: no remote copies, remote signals or barrier semaphores. Data moves between devices by JAX's collectives and lax.ppermute only.
A program may use at most 64 MiB of HBM per device.

```python
import jax
import jax.numpy as jnp
from jax import lax

BLK = 128
BLOCKS = 32
M = 4096


def draw_density(key, part):
    key = jax.random.fold_in(key, 1)
    gaussian = jax.random.normal(key, (M, M), jnp.float32)
    positions = jnp.arange(M)
    identity = (positions[:, None] == positions[None, :]).astype(jnp.float32)
    return (gaussian + gaussian.T) * (0.35 / jnp.sqrt(2.0 * M)) + 0.5 * identity


def draw_pattern(key, part):
    key = jax.random.fold_in(key, 2)
    picks = jax.random.randint(key, (BLOCKS, BLOCKS), 0, 3)
    kept = jnp.where(picks > 0, 1, 0)
    upper = jnp.maximum(kept, kept.T)
    positions = jnp.arange(BLOCKS)
    return jnp.where(positions[:, None] == positions[None, :], 1, upper).astype(jnp.int32)


def setup_inputs(seed: int = 0) -> dict:
    seeds = jax.random.split(jax.random.key(seed), 3)
    density = draw_density(jax.random.fold_in(seeds[2], 71), 0)
    pattern = draw_pattern(jax.random.fold_in(seeds[2], 71), 0)
    return {"density": density, "pattern": pattern}


def reference(density, pattern):
    expanded = jnp.repeat(jnp.repeat(pattern, BLK, 0), BLK, 1)
    masked = density * expanded.astype(jnp.float32)
    square = jnp.dot(masked, masked, precision=lax.Precision.HIGHEST, preferred_element_type=jnp.float32)
    cube = jnp.dot(square, masked, precision=lax.Precision.HIGHEST, preferred_element_type=jnp.float32)
    return square, 3.0 * square - 2.0 * cube
```

```python
import jax
import jax.numpy as jnp
from jax import lax
from jax.experimental import pallas as pl
from jax.experimental.pallas import tpu as pltpu
from jax.sharding import PartitionSpec as P

BLK = 128
SPAN = 4


def plane_permute(value, target):
    pairs = []
    for row in range(4):
        for x in range(4):
            for low in range(2):
                for core in range(2):
                    to = target(row, x, low, core)
                    pairs.append(
                        (
                            row * 16 + x * 4 + low * 2 + core,
                            to[0] * 16 + to[1] * 4 + to[2] * 2 + to[3],
                        )
                    )
    return lax.ppermute(value, ("row", "col"), pairs)


def split(value):
    high = value.astype(jnp.bfloat16)
    return high, (value - high.astype(jnp.float32)).astype(jnp.bfloat16)


def product_kernel(own_own, other_own, own_other, other_other, right, out):
    col = lax.axis_index("col")
    low, core = lax.rem(lax.div(col, 2), 2), lax.rem(col, 2)
    lefts = ((own_own, 0, 0), (other_own, 1, 0), (own_other, 0, 1), (other_other, 1, 1))
    rows = 4 * BLK
    total = jnp.zeros((rows, 256), jnp.float32)
    for ref, low_step, core_step in lefts:
        q = lax.rem(low + low_step, 2) * 2 + lax.rem(core + core_step, 2)
        left_high, left_low = split(ref[...].reshape(rows, 256))
        right_high, right_low = split(right[pl.ds(pl.multiple_of(q * 256, 256), 256), :])
        for a, b in ((left_high, right_high), (left_high, right_low), (left_low, right_high)):
            total = total + jnp.dot(a, b, preferred_element_type=jnp.float32)
    out[...] = total.reshape(4, BLK, 256)


def product(lefts, right):
    return pl.pallas_call(
        product_kernel,
        out_shape=jax.ShapeDtypeStruct((4, BLK, 256), jnp.float32),
        in_specs=[pl.BlockSpec(memory_space=pltpu.VMEM)] * 5,
        out_specs=pl.BlockSpec(memory_space=pltpu.VMEM),
        compiler_params=pltpu.CompilerParams(vmem_limit_bytes=32 * 1024 * 1024),
        cost_estimate=pl.CostEstimate(
            flops=6 * 512 * 1024 * 256, bytes_accessed=7 * 512 * 1024, transcendentals=0
        ),
    )(*lefts, right)


def body(density, pattern):
    row, col, layer = (lax.axis_index(name) for name in ("row", "col", "layer"))
    kept = lax.dynamic_slice(pattern, (row * 8 + layer, col * 2), (1, 2)).astype(jnp.float32)
    masked = density * jnp.repeat(kept, BLK, axis=1)
    right = lax.all_gather(masked, "layer").reshape(8 * BLK, 256)
    near = plane_permute(masked, lambda r, x, low, core: (x, r, low, core))
    far = plane_permute(masked, lambda r, x, low, core: (x, r, 1 - low, core))
    lines = [[x * SPAN + q for x in range(4)] for q in range(SPAN)]
    near_all = lax.all_gather(near, "col", axis_index_groups=lines)
    far_all = lax.all_gather(far, "col", axis_index_groups=lines)
    swap = [(i, i ^ 1) for i in range(16)]
    lefts = (
        near_all,
        far_all,
        lax.ppermute(near_all, "col", swap),
        lax.ppermute(far_all, "col", swap),
    )
    square_terms = product(lefts, right)
    square = jnp.sum(lax.all_to_all(square_terms, "row", 0, 0), axis=0)
    square_right = lax.all_to_all(
        jnp.broadcast_to(square[None], (8, BLK, 256)), "layer", 0, 0
    ).reshape(8 * BLK, 256)
    cube_terms = product(lefts, square_right)
    cube = jnp.sum(lax.all_to_all(cube_terms, "row", 0, 0), axis=0)
    return (square, 3.0 * square - 2.0 * cube)


def solution(mesh):
    in_specs = (P(("row", "layer"), "col"), P())
    out_specs = (P(("row", "layer"), "col"), P(("row", "layer"), "col"))
    return jax.shard_map(body, mesh=mesh, in_specs=in_specs, out_specs=out_specs, check_vma=False)
```

```python
import jax
import jax.numpy as jnp
from jax import lax
from jax.experimental import pallas as pl
from jax.experimental.pallas import tpu as pltpu
from jax.sharding import PartitionSpec as P

BLK = 128
WIDTH = 256
NEAR = 8


def split(value):
    high = value.astype(jnp.bfloat16)
    return high, (value - high.astype(jnp.float32)).astype(jnp.bfloat16)


def product_kernel(own, other, panel, out):
    core = lax.rem(lax.axis_index("col"), 2)
    total_high = jnp.zeros((2 * BLK, WIDTH), jnp.float32)
    total_low = jnp.zeros((BLK, WIDTH), jnp.float32)
    for ref, core_step in ((own, 0), (other, 1)):
        q_core = lax.rem(core + core_step, 2)
        for low in range(2):
            for x in range(4):
                left_high, left_low = split(ref[x * 2 + low])
                right = panel[pl.ds(4 * low + 2 * q_core, 2), x].reshape(2 * BLK, WIDTH)
                right_high, right_low = split(right)
                both = jnp.concatenate([left_high, left_low], axis=0)
                total_high += jnp.dot(both, right_high, preferred_element_type=jnp.float32)
                total_low += jnp.dot(left_high, right_low, preferred_element_type=jnp.float32)
    out[...] = total_high[:BLK] + (total_high[BLK:] + total_low)


def product(own, other, panel):
    return pl.pallas_call(
        product_kernel,
        out_shape=jax.ShapeDtypeStruct((BLK, WIDTH), jnp.float32),
        in_specs=[pl.BlockSpec(memory_space=pltpu.VMEM)] * 3,
        out_specs=pl.BlockSpec(memory_space=pltpu.VMEM),
        compiler_params=pltpu.CompilerParams(vmem_limit_bytes=32 * 1024 * 1024),
        cost_estimate=pl.CostEstimate(
            flops=6 * BLK * 4096 * WIDTH, bytes_accessed=6 * 1024 * 1024, transcendentals=0
        ),
    )(own, other, panel)


def slab(block):
    groups = [[chip * 2 + core for chip in range(NEAR)] for core in range(2)]
    copies = jnp.broadcast_to(block[None], (NEAR, BLK, WIDTH))
    own = lax.all_to_all(copies, "col", 0, 0, axis_index_groups=groups)
    return own, lax.ppermute(own, "col", [(i, i ^ 1) for i in range(16)])


def body(density, pattern):
    row, col, layer = (lax.axis_index(name) for name in ("row", "col", "layer"))
    kept = lax.dynamic_slice(pattern, (row * 8 + layer, col * 2), (1, 2)).astype(jnp.float32)
    masked = density * jnp.repeat(kept, BLK, axis=1)
    panel = lax.all_gather(lax.all_gather(masked, "row"), "layer")
    square = product(*slab(masked), panel)
    cube = product(*slab(square), panel)
    return (square, 3.0 * square - 2.0 * cube)


def solution(mesh):
    in_specs = (P(("row", "layer"), "col"), P())
    out_specs = (P(("row", "layer"), "col"), P(("row", "layer"), "col"))
    return jax.shard_map(body, mesh=mesh, in_specs=in_specs, out_specs=out_specs, check_vma=False)
```

```python
import jax
import jax.numpy as jnp
from jax import lax
from jax.experimental import pallas as pl
from jax.experimental.pallas import tpu as pltpu
from jax.sharding import PartitionSpec as P

BLK = 128
HALF = 64
WIDTH = 256
ROWS = 4
NEAR = 8
LAYERS = 8


def split(value):
    high = value.astype(jnp.bfloat16)
    return high, (value - high.astype(jnp.float32)).astype(jnp.bfloat16)


def triple_dot(left, right, dims):
    left_high, left_low = split(left)
    right_high, right_low = split(right)
    total = lax.dot_general(left_high, right_low, dims, preferred_element_type=jnp.float32)
    total += lax.dot_general(left_low, right_high, dims, preferred_element_type=jnp.float32)
    return total + lax.dot_general(left_high, right_high, dims, preferred_element_type=jnp.float32)


def first_kernel(rows, own, other, out):
    left_own = rows[:, 0].reshape(ROWS * HALF, WIDTH)
    left_other = rows[:, 1].reshape(ROWS * HALF, WIDTH)
    dims = (((1,), (1,)), ((), ()))
    for pair in range(LAYERS // 2):
        span = pl.ds(pair * 2 * BLK, 2 * BLK)
        total = triple_dot(left_own, own[span, :], dims)
        total += triple_dot(left_other, other[span, :], dims)
        out[2 * pair] = total[:, :BLK]
        out[2 * pair + 1] = total[:, BLK:]


def second_kernel(square, own, other, out):
    dims = (((1,), (0,)), ((), ()))
    for side, panel in ((0, own), (1, other)):
        total = jnp.zeros((ROWS * HALF, WIDTH), jnp.float32)
        for pair in range(LAYERS // 2):
            left = jnp.concatenate([square[2 * pair], square[2 * pair + 1]], axis=1)
            total += triple_dot(left, panel[pl.ds(pair * 2 * BLK, 2 * BLK), :], dims)
        for row in range(ROWS):
            out[row, side] = total[row * HALF : (row + 1) * HALF]


def call(kernel, shape, *operands):
    return pl.pallas_call(
        kernel,
        out_shape=jax.ShapeDtypeStruct(shape, jnp.float32),
        in_specs=[pl.BlockSpec(memory_space=pltpu.VMEM)] * len(operands),
        out_specs=pl.BlockSpec(memory_space=pltpu.VMEM),
        compiler_params=pltpu.CompilerParams(vmem_limit_bytes=32 * 1024 * 1024),
        cost_estimate=pl.CostEstimate(
            flops=6 * 256 * 512 * 1024, bytes_accessed=4 * 1024 * 1024, transcendentals=0
        ),
    )(*operands)


def swap_core(value):
    return lax.ppermute(value, "col", [(i, i ^ 1) for i in range(16)])


def mirror_chunk(piece, turn, core, layer):
    pairs = []
    for r in range(4):
        for c in range(16):
            for z in range(LAYERS):
                i = 2 * (c % 2) + (z + turn) % 2
                to = (r * 16 + i * 4 + z // 2) * LAYERS + c // 2
                pairs.append(((r * 16 + c) * LAYERS + z, to))
    chunk = lax.dynamic_index_in_dim(piece, (layer + turn) % 2, 0, keepdims=False)
    return lax.ppermute(chunk, ("row", "col", "layer"), pairs)


def near_exchange(value):
    groups = [[chip * 2 + core for chip in range(NEAR)] for core in range(2)]
    return lax.all_to_all(value, "col", 0, 0, axis_index_groups=groups)


def copies(value, count):
    return jnp.broadcast_to(value[None], (count, *value.shape))


def join_halves(mine, received, core):
    low = jnp.where(core == 0, mine, received)
    high = jnp.where(core == 0, received, mine)
    return jnp.concatenate([low, high], axis=0)


def body(density, pattern):
    row, col, layer = (lax.axis_index(name) for name in ("row", "col", "layer"))
    x, core = col // 4, col % 2
    kept = lax.dynamic_slice(pattern, (row * 8 + layer, col * 2), (1, 2)).astype(jnp.float32)
    masked = density * jnp.repeat(kept, BLK, axis=1)

    own = lax.all_to_all(copies(masked, LAYERS), "layer", 0, 0).reshape(LAYERS * BLK, WIDTH)

    halves = masked.reshape(2, HALF, WIDTH)
    mine = lax.dynamic_index_in_dim(halves, core, 0, keepdims=False)
    theirs = lax.dynamic_index_in_dim(halves, 1 - core, 0, keepdims=False)
    rows = jnp.concatenate([mine, swap_core(theirs)], axis=0)
    rows = lax.all_gather(rows, "row").reshape(ROWS, 2, HALF, WIDTH)

    own, rows = lax.optimization_barrier((own, rows))
    other = swap_core(own)
    square_terms = call(first_kernel, (LAYERS, ROWS * HALF, BLK), rows, own, other)
    square_piece = jnp.sum(near_exchange(square_terms), axis=0)
    square_rows = near_exchange(copies(square_piece, NEAR))

    pieces = square_piece.reshape(2, 2, HALF, BLK)
    mine = lax.dynamic_index_in_dim(pieces, core, 0, keepdims=False)
    theirs = swap_core(lax.dynamic_index_in_dim(pieces, 1 - core, 0, keepdims=False))
    pieces = jnp.where(
        core == 0,
        jnp.concatenate([mine, theirs], axis=1),
        jnp.concatenate([theirs, mine], axis=1),
    )
    square_rows, pieces = lax.optimization_barrier((square_rows, pieces))
    first = mirror_chunk(pieces, 0, core, layer)
    second = mirror_chunk(pieces, 1, core, layer)

    cube_terms = call(second_kernel, (ROWS, 2, HALF, WIDTH), square_rows, own, other)
    cube = jnp.sum(lax.all_to_all(cube_terms, "row", 0, 0), axis=0)
    cube, first, second = lax.optimization_barrier((cube, first, second))
    cube_home = join_halves(cube[0], swap_core(cube[1]), core)

    even = x % 2 == 0
    square_home = jnp.concatenate(
        [jnp.where(even, first, second).T, jnp.where(even, second, first).T], axis=1
    )
    return (square_home, 3.0 * square_home - 2.0 * cube_home)


def solution(mesh):
    in_specs = (P(("row", "layer"), "col"), P())
    out_specs = (P(("row", "layer"), "col"), P(("row", "layer"), "col"))
    return jax.shard_map(body, mesh=mesh, in_specs=in_specs, out_specs=out_specs, check_vma=False)
```

```python
import jax
import jax.numpy as jnp
from jax import lax
from jax.experimental import pallas as pl
from jax.experimental.pallas import tpu as pltpu
from jax.sharding import PartitionSpec as P

BLK = 128
HALF = 64
WIDTH = 256
ROWS = 4
NEAR = 8
LAYERS = 8


def split(value):
    high = value.astype(jnp.bfloat16)
    return high, (value - high.astype(jnp.float32)).astype(jnp.bfloat16)


def triple_dot(left, right, dims):
    left_high, left_low = split(left)
    right_high, right_low = split(right)
    total = lax.dot_general(left_high, right_low, dims, preferred_element_type=jnp.float32)
    total += lax.dot_general(left_low, right_high, dims, preferred_element_type=jnp.float32)
    return total + lax.dot_general(left_high, right_high, dims, preferred_element_type=jnp.float32)


def first_kernel(rows, own, other, out):
    high = lax.div(lax.axis_index("layer"), 4)
    left_own = rows[:, 0].reshape(ROWS * HALF, WIDTH)
    left_other = rows[:, 1].reshape(ROWS * HALF, WIDTH)
    dims = (((1,), (1,)), ((), ()))
    for part in range(4):
        span = pl.ds(part * WIDTH, WIDTH)
        total = triple_dot(left_own, own[span, :], dims)
        total += triple_dot(left_other, other[span, :], dims)
        q, side = divmod(part, 2)
        for i in range(ROWS):
            out[2 * i + (q ^ high), :, side * WIDTH : (side + 1) * WIDTH] = total[
                i * HALF : (i + 1) * HALF
            ]


def second_kernel(square, own, other, out):
    high = lax.div(lax.axis_index("layer"), 4)
    core = lax.rem(lax.axis_index("col"), 2)
    dims = (((1,), (0,)), ((), ()))
    for side, panel in ((0, own), (1, other)):
        total = jnp.zeros((ROWS * HALF, WIDTH), jnp.float32)
        for part in range(4):
            q, half = divmod(part, 2)
            left = jnp.concatenate(
                [
                    square[2 * i + (q ^ high), :, half * WIDTH : (half + 1) * WIDTH]
                    for i in range(ROWS)
                ],
                axis=0,
            )
            total += triple_dot(left, panel[pl.ds(part * WIDTH, WIDTH), :], dims)
        for i in range(ROWS):
            out[i, lax.rem(core + side, 2)] = total[i * HALF : (i + 1) * HALF]


def finish_kernel(cube, first, second, square, purified):
    even = lax.rem(lax.axis_index("layer"), 2) == 0
    home = jnp.concatenate(
        [
            jnp.where(even, first[...], second[...]).T,
            jnp.where(even, second[...], first[...]).T,
        ],
        axis=1,
    )
    square[...] = home
    for c in range(2):
        rows = slice(c * HALF, (c + 1) * HALF)
        total = (cube[c] + cube[2 + c]) + (cube[4 + c] + cube[6 + c])
        purified[rows] = 3.0 * home[rows] - 2.0 * total


def mask_kernel(pattern, density, out, masked, sems):
    row = lax.axis_index("row") * LAYERS + lax.axis_index("layer")
    col = lax.axis_index("col")
    for h in range(2):
        kept = pattern[row, 2 * col + h].astype(jnp.float32)
        span = slice(h * BLK, (h + 1) * BLK)
        masked[:, span] = density[:, span] * kept
    sends = [pltpu.make_async_copy(masked, out.at[k], sems.at[k]) for k in range(LAYERS)]
    for send in sends:
        send.start()
    for send in sends:
        send.wait()


def masked_copies(pattern, density):
    return pl.pallas_call(
        mask_kernel,
        out_shape=(
            jax.ShapeDtypeStruct((LAYERS, BLK, WIDTH), jnp.float32),
            jax.ShapeDtypeStruct((BLK, WIDTH), jnp.float32),
        ),
        in_specs=[
            pl.BlockSpec(memory_space=pltpu.SMEM),
            pl.BlockSpec(memory_space=pltpu.VMEM),
        ],
        out_specs=(pl.BlockSpec(memory_space=pl.ANY), pl.BlockSpec(memory_space=pltpu.VMEM)),
        scratch_shapes=[pltpu.SemaphoreType.DMA((LAYERS,))],
        cost_estimate=pl.CostEstimate(
            flops=BLK * WIDTH, bytes_accessed=9 * BLK * WIDTH * 4, transcendentals=0
        ),
    )(pattern, density)


def call(kernel, shapes, *operands, flops=6 * 256 * 512 * 1024):
    return pl.pallas_call(
        kernel,
        out_shape=[jax.ShapeDtypeStruct(shape, jnp.float32) for shape in shapes],
        in_specs=[pl.BlockSpec(memory_space=pltpu.VMEM)] * len(operands),
        out_specs=[pl.BlockSpec(memory_space=pltpu.VMEM)] * len(shapes),
        compiler_params=pltpu.CompilerParams(vmem_limit_bytes=32 * 1024 * 1024),
        cost_estimate=pl.CostEstimate(
            flops=flops, bytes_accessed=1024 * 1024, transcendentals=0
        ),
    )(*operands)


def swap_core(value):
    return lax.ppermute(value, "col", [(i, i ^ 1) for i in range(16)])


def near_exchange(value):
    groups = [[chip * 2 + core for chip in range(NEAR)] for core in range(2)]
    return lax.all_to_all(value, "col", 0, 0, axis_index_groups=groups)


def copies(value, count):
    return jnp.broadcast_to(value[None], (count, *value.shape))


def mirror_home(piece, turn, layer):
    pairs = []
    for r in range(4):
        for c in range(16):
            for z in range(LAYERS):
                to = (r * 16 + c // 4 * 4 + z // 2) * LAYERS + (z ^ (2 * (c % 4) + turn))
                pairs.append(((r * 16 + c) * LAYERS + z, to))
    return lax.ppermute(piece[turn], ("row", "col", "layer"), pairs)


def whole_rows(piece, core, layer):
    blocks = [piece[:, k * BLK : (k + 1) * BLK] for k in range(4)]
    blocks = jnp.stack(blocks)
    pick = lambda c: jnp.stack(
        [
            lax.dynamic_index_in_dim(blocks, (layer % 4) ^ (2 * c + j), 0, keepdims=False)
            for j in range(2)
        ]
    )
    mine, theirs = pick(core), swap_core(pick(1 - core))
    return jnp.where(
        core == 0,
        jnp.concatenate([mine, theirs], axis=1),
        jnp.concatenate([theirs, mine], axis=1),
    )


def body(density, pattern):
    core = lax.axis_index("col") % 2
    sends, masked = masked_copies(pattern, density)

    own = lax.all_to_all(sends, "layer", 0, 0).reshape(LAYERS * BLK, WIDTH)

    halves = masked.reshape(2, HALF, WIDTH)
    mine = lax.dynamic_index_in_dim(halves, core, 0, keepdims=False)
    theirs = lax.dynamic_index_in_dim(halves, 1 - core, 0, keepdims=False)
    rows = jnp.concatenate([mine, swap_core(theirs)], axis=0)
    rows = lax.all_gather(rows, "row").reshape(ROWS, 2, HALF, WIDTH)

    own, rows = lax.optimization_barrier((own, rows))
    other = swap_core(own)
    (square_terms,) = call(first_kernel, [(NEAR, HALF, 2 * WIDTH)], rows, own, other)
    square_piece = jnp.sum(near_exchange(square_terms), axis=0)
    square_rows = near_exchange(copies(square_piece, NEAR))
    layer = lax.axis_index("layer")
    piece = whole_rows(square_piece, core, layer)
    square_rows, piece = lax.optimization_barrier((square_rows, piece))
    first, second = mirror_home(piece, 0, layer), mirror_home(piece, 1, layer)

    (cube_terms,) = call(second_kernel, [(ROWS, 2, HALF, WIDTH)], square_rows, own, other)
    homes = [
        [r * 16 + chip * 2 + c for r in range(ROWS) for c in range(2)] for chip in range(NEAR)
    ]
    cube_terms = cube_terms.reshape(ROWS * 2, HALF, WIDTH)
    cube = lax.all_to_all(cube_terms, ("row", "col"), 0, 0, axis_index_groups=homes)
    cube, first, second = lax.optimization_barrier((cube, first, second))
    square, purified = call(
        finish_kernel, [(BLK, WIDTH)] * 2, cube, first, second, flops=16 * BLK * WIDTH
    )
    return (square, purified)


def solution(mesh):
    in_specs = (P(("row", "layer"), "col"), P())
    out_specs = (P(("row", "layer"), "col"), P(("row", "layer"), "col"))
    return jax.shard_map(body, mesh=mesh, in_specs=in_specs, out_specs=out_specs, check_vma=False)
```

```python
import jax
import jax.numpy as jnp
from jax import lax
from jax.experimental import pallas as pl
from jax.experimental.pallas import tpu as pltpu
from jax.sharding import PartitionSpec as P

BLK = 128
HALF = 64
WIDTH = 256
ROWS = 4
NEAR = 8
LAYERS = 8


def split(value):
    high = value.astype(jnp.bfloat16)
    return high, (value - high.astype(jnp.float32)).astype(jnp.bfloat16)


def triple_dot(left, right, dims):
    left_high, left_low = split(left)
    right_high, right_low = split(right)
    total = lax.dot_general(left_high, right_low, dims, preferred_element_type=jnp.float32)
    total += lax.dot_general(left_low, right_high, dims, preferred_element_type=jnp.float32)
    return total + lax.dot_general(left_high, right_high, dims, preferred_element_type=jnp.float32)


def first_kernel(rows, own, other, rows_kept, panel_kept, out):
    high = lax.div(lax.axis_index("layer"), 4)
    lefts = [
        jnp.concatenate(
            [rows[i, side] * rows_kept[side, i : i + 1, :] for i in range(ROWS)], axis=0
        )
        for side in range(2)
    ]
    dims = (((1,), (1,)), ((), ()))
    for part in range(4):
        total = triple_dot(lefts[0], panel_part(own, panel_kept, 0, part), dims)
        total += triple_dot(lefts[1], panel_part(other, panel_kept, 1, part), dims)
        q, half = divmod(part, 2)
        for i in range(ROWS):
            out[2 * i + (q ^ high), :, half * WIDTH : (half + 1) * WIDTH] = total[
                i * HALF : (i + 1) * HALF
            ]


def panel_part(panel, kept, side, part):
    return jnp.concatenate(
        [panel[z * BLK : (z + 1) * BLK, :] * kept[side, z : z + 1, :] for z in (2 * part, 2 * part + 1)],
        axis=0,
    )


def second_kernel(square, own, other, panel_kept, out):
    high = lax.div(lax.axis_index("layer"), 4)
    core = lax.rem(lax.axis_index("col"), 2)
    dims = (((1,), (0,)), ((), ()))
    for side, panel in ((0, own), (1, other)):
        total = jnp.zeros((ROWS * HALF, WIDTH), jnp.float32)
        for part in range(4):
            q, half = divmod(part, 2)
            left = jnp.concatenate(
                [
                    square[2 * i + (q ^ high), :, half * WIDTH : (half + 1) * WIDTH]
                    for i in range(ROWS)
                ],
                axis=0,
            )
            total += triple_dot(left, panel_part(panel, panel_kept, side, part), dims)
        for i in range(ROWS):
            out[i, lax.rem(core + side, 2)] = total[i * HALF : (i + 1) * HALF]


def finish_kernel(cube, mirrored, square, purified):
    home = mirrored[...].T
    square[...] = home
    for c in range(2):
        rows = slice(c * HALF, (c + 1) * HALF)
        total = (cube[c] + cube[2 + c]) + (cube[4 + c] + cube[6 + c])
        purified[rows] = 3.0 * home[rows] - 2.0 * total


def call(kernel, shapes, *operands, flops):
    return pl.pallas_call(
        kernel,
        out_shape=[jax.ShapeDtypeStruct(shape, jnp.float32) for shape in shapes],
        in_specs=[pl.BlockSpec(memory_space=pltpu.VMEM)] * len(operands),
        out_specs=[pl.BlockSpec(memory_space=pltpu.VMEM)] * len(shapes),
        compiler_params=pltpu.CompilerParams(vmem_limit_bytes=32 * 1024 * 1024),
        cost_estimate=pl.CostEstimate(
            flops=flops, bytes_accessed=1024 * 1024, transcendentals=0
        ),
    )(*operands)


def kept_columns(pattern, col):
    both = [lax.dynamic_slice_in_dim(pattern, 2 * (col ^ side), 2, axis=1) for side in range(2)]
    return jnp.repeat(jnp.stack(both).astype(jnp.float32), BLK, axis=2)


def swap_core(value):
    return lax.ppermute(value, "col", [(i, i ^ 1) for i in range(16)])


def near_exchange(value):
    groups = [[chip * 2 + core for chip in range(NEAR)] for core in range(2)]
    return lax.all_to_all(value, "col", 0, 0, axis_index_groups=groups)


def copies(value, count):
    return jnp.broadcast_to(value[None], (count, *value.shape))


def mirror_home(piece):
    pairs = []
    for r in range(4):
        for c in range(16):
            for z in range(LAYERS):
                to = (r * 16 + c // 4 * 4 + z // 2) * LAYERS + (z ^ (2 * (c % 4)))
                pairs.append(((r * 16 + c) * LAYERS + z, to))
    return lax.ppermute(piece, ("row", "col", "layer"), pairs)


def layer_pair(pieces, layer):
    received = lax.ppermute(pieces[1], "layer", [(z, z ^ 1) for z in range(LAYERS)])
    return jnp.where(
        layer % 2 == 0,
        jnp.concatenate([pieces[0], received], axis=0),
        jnp.concatenate([received, pieces[0]], axis=0),
    )


def whole_rows(piece, core, layer):
    blocks = [piece[:, k * BLK : (k + 1) * BLK] for k in range(4)]
    blocks = jnp.stack(blocks)
    pick = lambda c: jnp.stack(
        [
            lax.dynamic_index_in_dim(blocks, (layer % 4) ^ (2 * c + j), 0, keepdims=False)
            for j in range(2)
        ]
    )
    mine, theirs = pick(core), swap_core(pick(1 - core))
    return jnp.where(
        core == 0,
        jnp.concatenate([mine, theirs], axis=1),
        jnp.concatenate([theirs, mine], axis=1),
    )


def body(density, pattern):
    row, col, layer = (lax.axis_index(name) for name in ("row", "col", "layer"))
    core = col % 2
    row_groups = pattern.reshape(ROWS, LAYERS, ROWS * LAYERS)
    panel_kept = kept_columns(lax.dynamic_index_in_dim(row_groups, row, 0, keepdims=False), col)
    rows_kept = kept_columns(lax.dynamic_index_in_dim(row_groups, layer, 1, keepdims=False), col)

    own = lax.all_to_all(copies(density, LAYERS), "layer", 0, 0).reshape(LAYERS * BLK, WIDTH)

    halves = density.reshape(2, HALF, WIDTH)
    mine = lax.dynamic_index_in_dim(halves, core, 0, keepdims=False)
    theirs = lax.dynamic_index_in_dim(halves, 1 - core, 0, keepdims=False)
    rows = jnp.concatenate([mine, swap_core(theirs)], axis=0)
    rows = lax.all_gather(rows, "row").reshape(ROWS, 2, HALF, WIDTH)

    own, rows = lax.optimization_barrier((own, rows))
    other = swap_core(own)
    flops = 6 * 256 * 512 * 1024
    (square_terms,) = call(
        first_kernel,
        [(NEAR, HALF, 2 * WIDTH)],
        rows,
        own,
        other,
        rows_kept,
        panel_kept,
        flops=flops,
    )
    square_piece = jnp.sum(near_exchange(square_terms), axis=0)
    square_rows = near_exchange(copies(square_piece, NEAR))
    piece = layer_pair(whole_rows(square_piece, core, layer), layer)
    square_rows, piece = lax.optimization_barrier((square_rows, piece))
    mirrored = mirror_home(piece)

    (cube_terms,) = call(
        second_kernel,
        [(ROWS, 2, HALF, WIDTH)],
        square_rows,
        own,
        other,
        panel_kept,
        flops=flops,
    )
    homes = [
        [r * 16 + chip * 2 + c for r in range(ROWS) for c in range(2)] for chip in range(NEAR)
    ]
    cube_terms = cube_terms.reshape(ROWS * 2, HALF, WIDTH)
    cube = lax.all_to_all(cube_terms, ("row", "col"), 0, 0, axis_index_groups=homes)
    cube, mirrored = lax.optimization_barrier((cube, mirrored))
    square, purified = call(
        finish_kernel, [(BLK, WIDTH)] * 2, cube, mirrored, flops=16 * BLK * WIDTH
    )
    return (square, purified)


def solution(mesh):
    in_specs = (P(("row", "layer"), "col"), P())
    out_specs = (P(("row", "layer"), "col"), P(("row", "layer"), "col"))
    return jax.shard_map(body, mesh=mesh, in_specs=in_specs, out_specs=out_specs, check_vma=False)
```

```python
import jax
import jax.numpy as jnp
from jax import lax
from jax.experimental import pallas as pl
from jax.experimental.pallas import tpu as pltpu
from jax.sharding import PartitionSpec as P

BLK = 128
HALF = 64
WIDTH = 256
ROWS = 4
NEAR = 8
LAYERS = 8


def split(value):
    high = value.astype(jnp.bfloat16)
    return high, (value - high.astype(jnp.float32)).astype(jnp.bfloat16)


def triple_dot(left, right, dims):
    left_high, left_low = split(left)
    right_high, right_low = split(right)
    total = lax.dot_general(left_high, right_low, dims, preferred_element_type=jnp.float32)
    total += lax.dot_general(left_low, right_high, dims, preferred_element_type=jnp.float32)
    return total + lax.dot_general(left_high, right_high, dims, preferred_element_type=jnp.float32)


def first_kernel(rows, own, other, rows_kept, panel_kept, out):
    high = lax.div(lax.axis_index("layer"), 4)
    turn = 4 * lax.rem(lax.axis_index("col"), 2)
    lefts = [
        jnp.concatenate(
            [rows[i, side] * rows_kept[side, i : i + 1, :] for i in range(ROWS)], axis=0
        )
        for side in range(2)
    ]
    dims = (((1,), (1,)), ((), ()))
    for part in range(4):
        total = triple_dot(lefts[0], panel_part(own, panel_kept, 0, part), dims)
        total += triple_dot(lefts[1], panel_part(other, panel_kept, 1, part), dims)
        q, half = divmod(part, 2)
        for i in range(ROWS):
            out[(2 * i + (q ^ high)) ^ turn, :, half * WIDTH : (half + 1) * WIDTH] = total[
                i * HALF : (i + 1) * HALF
            ]


def panel_part(panel, kept, side, part):
    turn = 4 * ((lax.rem(lax.axis_index("col"), 2) + side) % 2)
    start = pl.multiple_of(((2 * part) ^ turn) * BLK, 2 * BLK)
    blocks = panel[pl.ds(start, 2 * BLK), :]
    return jnp.concatenate(
        [blocks[h * BLK : (h + 1) * BLK] * kept[side, 2 * part + h : 2 * part + h + 1, :] for h in range(2)],
        axis=0,
    )


def second_kernel(square, own, other, panel_kept, out):
    high = lax.div(lax.axis_index("layer"), 4)
    core = lax.rem(lax.axis_index("col"), 2)
    turn = 4 * core
    first = 2 * (1 - lax.rem(lax.div(lax.axis_index("col"), 2), 2))
    dims = (((1,), (0,)), ((), ()))
    for side, panel in ((0, own), (1, other)):
        total = jnp.zeros((ROWS * HALF, WIDTH), jnp.float32)
        for part in range(4):
            q, half = divmod(part, 2)
            left = jnp.concatenate(
                [
                    square[(2 * i + (q ^ high)) ^ turn, :, half * WIDTH : (half + 1) * WIDTH]
                    for i in range(ROWS)
                ],
                axis=0,
            )
            total += triple_dot(left, panel_part(panel, panel_kept, side, part), dims)
        for i in range(ROWS):
            out[lax.rem(i + first, ROWS), lax.rem(core + side, 2)] = total[i * HALF : (i + 1) * HALF]


def finish_kernel(cube, mirrored, square, purified):
    home = mirrored[...].T
    square[...] = home
    for c in range(2):
        rows = slice(c * HALF, (c + 1) * HALF)
        total = (cube[c] + cube[2 + c]) + (cube[4 + c] + cube[6 + c])
        purified[rows] = 3.0 * home[rows] - 2.0 * total


def call(kernel, shapes, *operands, flops):
    return pl.pallas_call(
        kernel,
        out_shape=[jax.ShapeDtypeStruct(shape, jnp.float32) for shape in shapes],
        in_specs=[pl.BlockSpec(memory_space=pltpu.VMEM)] * len(operands),
        out_specs=[pl.BlockSpec(memory_space=pltpu.VMEM)] * len(shapes),
        compiler_params=pltpu.CompilerParams(vmem_limit_bytes=32 * 1024 * 1024),
        cost_estimate=pl.CostEstimate(
            flops=flops, bytes_accessed=1024 * 1024, transcendentals=0
        ),
    )(*operands)


def kept_columns(pattern, col):
    both = [lax.dynamic_slice_in_dim(pattern, 2 * (col ^ side), 2, axis=1) for side in range(2)]
    return jnp.repeat(jnp.stack(both).astype(jnp.float32), BLK, axis=2)


def swap_core(value):
    return lax.ppermute(value, "col", [(i, i ^ 1) for i in range(16)])


def near_exchange(value):
    groups = [[(chip ^ 4 * core) * 2 + core for chip in range(NEAR)] for core in range(2)]
    return lax.all_to_all(value, "col", 0, 0, axis_index_groups=groups)


def copies(value, count):
    return jnp.broadcast_to(value[None], (count, *value.shape))


def mirror_home(piece):
    pairs = []
    for r in range(4):
        for c in range(16):
            for z in range(LAYERS):
                to = (r * 16 + c // 4 * 4 + z // 2) * LAYERS + (z ^ (2 * (c % 4)))
                pairs.append(((r * 16 + c) * LAYERS + z, to))
    return lax.ppermute(piece, ("row", "col", "layer"), pairs)


def layer_pair(pieces, layer):
    received = lax.ppermute(pieces[1], "layer", [(z, z ^ 1) for z in range(LAYERS)])
    return jnp.where(
        layer % 2 == 0,
        jnp.concatenate([pieces[0], received], axis=0),
        jnp.concatenate([received, pieces[0]], axis=0),
    )


def whole_rows(piece, core, layer):
    blocks = [piece[:, k * BLK : (k + 1) * BLK] for k in range(4)]
    blocks = jnp.stack(blocks)
    pick = lambda c: jnp.stack(
        [
            lax.dynamic_index_in_dim(blocks, (layer % 4) ^ (2 * c + j), 0, keepdims=False)
            for j in range(2)
        ]
    )
    mine, theirs = pick(core), swap_core(pick(1 - core))
    return jnp.where(
        core == 0,
        jnp.concatenate([mine, theirs], axis=1),
        jnp.concatenate([theirs, mine], axis=1),
    )


def body(density, pattern):
    row, col, layer = (lax.axis_index(name) for name in ("row", "col", "layer"))
    core = col % 2
    row_groups = pattern.reshape(ROWS, LAYERS, ROWS * LAYERS)
    panel_kept = kept_columns(lax.dynamic_index_in_dim(row_groups, row, 0, keepdims=False), col)
    rows_kept = kept_columns(lax.dynamic_index_in_dim(row_groups, layer, 1, keepdims=False), col)

    lines = [[c * LAYERS + (z ^ 4 * (c % 2)) for z in range(LAYERS)] for c in range(16)]
    own = lax.all_to_all(
        copies(density, LAYERS), ("col", "layer"), 0, 0, axis_index_groups=lines
    ).reshape(LAYERS * BLK, WIDTH)

    halves = density.reshape(2, HALF, WIDTH)
    mine = lax.dynamic_index_in_dim(halves, core, 0, keepdims=False)
    theirs = lax.dynamic_index_in_dim(halves, 1 - core, 0, keepdims=False)
    rows = jnp.concatenate([mine, swap_core(theirs)], axis=0)
    rows = lax.all_gather(rows, "row").reshape(ROWS, 2, HALF, WIDTH)

    own, rows = lax.optimization_barrier((own, rows))
    other = swap_core(own)
    flops = 6 * 256 * 512 * 1024
    (square_terms,) = call(
        first_kernel,
        [(NEAR, HALF, 2 * WIDTH)],
        rows,
        own,
        other,
        rows_kept,
        panel_kept,
        flops=flops,
    )
    square_piece = jnp.sum(near_exchange(square_terms), axis=0)
    square_rows = near_exchange(copies(square_piece, NEAR))
    piece = layer_pair(whole_rows(square_piece, core, layer), layer)
    square_rows, piece = lax.optimization_barrier((square_rows, piece))
    mirrored = mirror_home(piece)

    (cube_terms,) = call(
        second_kernel,
        [(ROWS, 2, HALF, WIDTH)],
        square_rows,
        own,
        other,
        panel_kept,
        flops=flops,
    )
    homes = [
        [(r + 2 * (1 - chip % 2)) % ROWS * 16 + chip * 2 + c for r in range(ROWS) for c in range(2)]
        for chip in range(NEAR)
    ]
    cube_terms = cube_terms.reshape(ROWS * 2, HALF, WIDTH)
    cube = lax.all_to_all(cube_terms, ("row", "col"), 0, 0, axis_index_groups=homes)
    cube, mirrored = lax.optimization_barrier((cube, mirrored))
    square, purified = call(
        finish_kernel, [(BLK, WIDTH)] * 2, cube, mirrored, flops=16 * BLK * WIDTH
    )
    return (square, purified)


def solution(mesh):
    in_specs = (P(("row", "layer"), "col"), P())
    out_specs = (P(("row", "layer"), "col"), P(("row", "layer"), "col"))
    return jax.shard_map(body, mesh=mesh, in_specs=in_specs, out_specs=out_specs, check_vma=False)
```

```python
import jax
import jax.numpy as jnp
from jax import lax
from jax.experimental import pallas as pl
from jax.experimental.pallas import tpu as pltpu
from jax.sharding import PartitionSpec as P

BLK = 128
HALF = 64
WIDTH = 256
ROWS = 4
NEAR = 8
LAYERS = 8


def split(value):
    high = value.astype(jnp.bfloat16)
    return high, (value - high.astype(jnp.float32)).astype(jnp.bfloat16)


def triple_dot(left, right, dims):
    left_high, left_low = split(left)
    right_high, right_low = split(right)
    total = lax.dot_general(left_high, right_low, dims, preferred_element_type=jnp.float32)
    total += lax.dot_general(left_low, right_high, dims, preferred_element_type=jnp.float32)
    return total + lax.dot_general(left_high, right_high, dims, preferred_element_type=jnp.float32)


def first_terms(rows, panel, rows_kept, panel_kept, side, part):
    left = jnp.concatenate(
        [rows[i, side] * rows_kept[side, i : i + 1, :] for i in range(ROWS)], axis=0
    )
    dims = (((1,), (1,)), ((), ()))
    return triple_dot(left, panel_part(panel, panel_kept, side, part), dims)


def own_kernel(rows, own, rows_kept, panel_kept, out):
    for part in range(4):
        out[part] = first_terms(rows, own, rows_kept, panel_kept, 0, part)


def first_kernel(rows, begun, other, rows_kept, panel_kept, out):
    high = lax.div(lax.axis_index("layer"), 4)
    turn = 4 * lax.rem(lax.axis_index("col"), 2)
    for part in range(4):
        total = begun[part] + first_terms(rows, other, rows_kept, panel_kept, 1, part)
        q, half = divmod(part, 2)
        for i in range(ROWS):
            out[(2 * i + (q ^ high)) ^ turn, :, half * WIDTH : (half + 1) * WIDTH] = total[
                i * HALF : (i + 1) * HALF
            ]


def panel_part(panel, kept, side, part):
    turn = 4 * ((lax.rem(lax.axis_index("col"), 2) + side) % 2)
    start = pl.multiple_of(((2 * part) ^ turn) * BLK, 2 * BLK)
    blocks = panel[pl.ds(start, 2 * BLK), :]
    return jnp.concatenate(
        [blocks[h * BLK : (h + 1) * BLK] * kept[side, 2 * part + h : 2 * part + h + 1, :] for h in range(2)],
        axis=0,
    )


def second_kernel(square, own, other, panel_kept, out):
    high = lax.div(lax.axis_index("layer"), 4)
    core = lax.rem(lax.axis_index("col"), 2)
    turn = 4 * core
    first = 2 * (1 - lax.rem(lax.div(lax.axis_index("col"), 2), 2))
    dims = (((1,), (0,)), ((), ()))
    for side, panel in ((0, own), (1, other)):
        total = jnp.zeros((ROWS * HALF, WIDTH), jnp.float32)
        for part in range(4):
            q, half = divmod(part, 2)
            left = jnp.concatenate(
                [
                    square[(2 * i + (q ^ high)) ^ turn, :, half * WIDTH : (half + 1) * WIDTH]
                    for i in range(ROWS)
                ],
                axis=0,
            )
            total += triple_dot(left, panel_part(panel, panel_kept, side, part), dims)
        for i in range(ROWS):
            out[lax.rem(i + first, ROWS), lax.rem(core + side, 2)] = total[i * HALF : (i + 1) * HALF]


def home_kernel(mirrored, square):
    square[...] = mirrored[...].T


def finish_kernel(cube, square, purified):
    for c in range(2):
        rows = slice(c * HALF, (c + 1) * HALF)
        total = (cube[c] + cube[2 + c]) + (cube[4 + c] + cube[6 + c])
        purified[rows] = 3.0 * square[rows] - 2.0 * total


def call(kernel, shapes, *operands, flops):
    return pl.pallas_call(
        kernel,
        out_shape=[jax.ShapeDtypeStruct(shape, jnp.float32) for shape in shapes],
        in_specs=[pl.BlockSpec(memory_space=pltpu.VMEM)] * len(operands),
        out_specs=[pl.BlockSpec(memory_space=pltpu.VMEM)] * len(shapes),
        compiler_params=pltpu.CompilerParams(vmem_limit_bytes=32 * 1024 * 1024),
        cost_estimate=pl.CostEstimate(
            flops=flops, bytes_accessed=1024 * 1024, transcendentals=0
        ),
    )(*operands)


def kept_columns(pattern, col):
    both = [lax.dynamic_slice_in_dim(pattern, 2 * (col ^ side), 2, axis=1) for side in range(2)]
    return jnp.repeat(jnp.stack(both).astype(jnp.float32), BLK, axis=2)


def swap_core(value):
    return lax.ppermute(value, "col", [(i, i ^ 1) for i in range(16)])


def near_exchange(value):
    groups = [[(chip ^ 4 * core) * 2 + core for chip in range(NEAR)] for core in range(2)]
    return lax.all_to_all(value, "col", 0, 0, axis_index_groups=groups)


def copies(value, count):
    return jnp.broadcast_to(value[None], (count, *value.shape))


def mirror_home(piece):
    pairs = []
    for r in range(4):
        for c in range(16):
            for z in range(LAYERS):
                to = (r * 16 + c // 4 * 4 + z // 2) * LAYERS + (z ^ (2 * (c % 4)))
                pairs.append(((r * 16 + c) * LAYERS + z, to))
    return lax.ppermute(piece, ("row", "col", "layer"), pairs)


def layer_pair(pieces, layer):
    received = lax.ppermute(pieces[1], "layer", [(z, z ^ 1) for z in range(LAYERS)])
    return jnp.where(
        layer % 2 == 0,
        jnp.concatenate([pieces[0], received], axis=0),
        jnp.concatenate([received, pieces[0]], axis=0),
    )


def whole_rows(piece, core, layer):
    blocks = [piece[:, k * BLK : (k + 1) * BLK] for k in range(4)]
    blocks = jnp.stack(blocks)
    pick = lambda c: jnp.stack(
        [
            lax.dynamic_index_in_dim(blocks, (layer % 4) ^ (2 * c + j), 0, keepdims=False)
            for j in range(2)
        ]
    )
    mine, theirs = pick(core), swap_core(pick(1 - core))
    return jnp.where(
        core == 0,
        jnp.concatenate([mine, theirs], axis=1),
        jnp.concatenate([theirs, mine], axis=1),
    )


def body(density, pattern):
    row, col, layer = (lax.axis_index(name) for name in ("row", "col", "layer"))
    core = col % 2
    row_groups = pattern.reshape(ROWS, LAYERS, ROWS * LAYERS)
    panel_kept = kept_columns(lax.dynamic_index_in_dim(row_groups, row, 0, keepdims=False), col)
    rows_kept = kept_columns(lax.dynamic_index_in_dim(row_groups, layer, 1, keepdims=False), col)

    lines = [[c * LAYERS + (z ^ 4 * (c % 2)) for z in range(LAYERS)] for c in range(16)]
    own = lax.all_to_all(
        copies(density, LAYERS), ("col", "layer"), 0, 0, axis_index_groups=lines
    ).reshape(LAYERS * BLK, WIDTH)

    halves = density.reshape(2, HALF, WIDTH)
    mine = lax.dynamic_index_in_dim(halves, core, 0, keepdims=False)
    theirs = lax.dynamic_index_in_dim(halves, 1 - core, 0, keepdims=False)
    rows = jnp.concatenate([mine, swap_core(theirs)], axis=0)
    rows = lax.all_gather(rows, "row").reshape(ROWS, 2, HALF, WIDTH)

    own, rows = lax.optimization_barrier((own, rows))
    other = swap_core(own)
    flops = 6 * 256 * 512 * 1024
    (begun,) = call(
        own_kernel,
        [(4, ROWS * HALF, WIDTH)],
        rows,
        own,
        rows_kept,
        panel_kept,
        flops=flops // 2,
    )
    (square_terms,) = call(
        first_kernel,
        [(NEAR, HALF, 2 * WIDTH)],
        rows,
        begun,
        other,
        rows_kept,
        panel_kept,
        flops=flops // 2,
    )
    square_piece = jnp.sum(near_exchange(square_terms), axis=0)
    square_rows = near_exchange(copies(square_piece, NEAR))
    piece = layer_pair(whole_rows(square_piece, core, layer), layer)
    square_rows, piece = lax.optimization_barrier((square_rows, piece))
    mirrored = mirror_home(piece)

    (cube_terms,) = call(
        second_kernel,
        [(ROWS, 2, HALF, WIDTH)],
        square_rows,
        own,
        other,
        panel_kept,
        flops=flops,
    )
    homes = [
        [(r + 2 * (1 - chip % 2)) % ROWS * 16 + chip * 2 + c for r in range(ROWS) for c in range(2)]
        for chip in range(NEAR)
    ]
    cube_terms = cube_terms.reshape(ROWS * 2, HALF, WIDTH)
    cube = lax.all_to_all(cube_terms, ("row", "col"), 0, 0, axis_index_groups=homes)
    (square,) = call(home_kernel, [(BLK, WIDTH)], mirrored, flops=BLK * WIDTH)
    cube, square = lax.optimization_barrier((cube, square))
    (purified,) = call(finish_kernel, [(BLK, WIDTH)], cube, square, flops=8 * BLK * WIDTH)
    return (square, purified)


def solution(mesh):
    in_specs = (P(("row", "layer"), "col"), P())
    out_specs = (P(("row", "layer"), "col"), P(("row", "layer"), "col"))
    return jax.shard_map(body, mesh=mesh, in_specs=in_specs, out_specs=out_specs, check_vma=False)
```

```python
import jax
import jax.numpy as jnp
from jax import lax
from jax.experimental import pallas as pl
from jax.experimental.pallas import tpu as pltpu
from jax.sharding import PartitionSpec as P

BLK = 128
HALF = 64
WIDTH = 256
ROWS = 4
NEAR = 8
LAYERS = 8


def split(value):
    high = value.astype(jnp.bfloat16)
    return high, (value - high.astype(jnp.float32)).astype(jnp.bfloat16)


def triple_dot(left, right, dims):
    left_high, left_low = split(left)
    right_high, right_low = split(right)
    total = lax.dot_general(left_high, right_low, dims, preferred_element_type=jnp.float32)
    total += lax.dot_general(left_low, right_high, dims, preferred_element_type=jnp.float32)
    return total + lax.dot_general(left_high, right_high, dims, preferred_element_type=jnp.float32)


def first_kernel(rows, own, other, rows_kept, panel_kept, out):
    high = lax.div(lax.axis_index("layer"), 4)
    turn = 4 * lax.rem(lax.axis_index("col"), 2)
    lefts = [
        jnp.concatenate(
            [rows[i, side] * rows_kept[side, i : i + 1, :] for i in range(ROWS)], axis=0
        )
        for side in range(2)
    ]
    dims = (((1,), (1,)), ((), ()))
    for part in range(4):
        total = triple_dot(lefts[0], panel_part(own, panel_kept, 0, part), dims)
        total += triple_dot(lefts[1], panel_part(other, panel_kept, 1, part), dims)
        q, half = divmod(part, 2)
        for i in range(ROWS):
            out[(2 * i + (q ^ high)) ^ turn, :, half * WIDTH : (half + 1) * WIDTH] = total[
                i * HALF : (i + 1) * HALF
            ]


def panel_part(panel, kept, side, part):
    turn = 4 * ((lax.rem(lax.axis_index("col"), 2) + side + 1) % 2)
    start = pl.multiple_of(((2 * part) ^ turn) * BLK, 2 * BLK)
    blocks = panel[pl.ds(start, 2 * BLK), :]
    return jnp.concatenate(
        [blocks[h * BLK : (h + 1) * BLK] * kept[side, 2 * part + h : 2 * part + h + 1, :] for h in range(2)],
        axis=0,
    )


def second_kernel(square, own, other, panel_kept, out):
    high = lax.div(lax.axis_index("layer"), 4)
    core = lax.rem(lax.axis_index("col"), 2)
    turn = 4 * core
    first = 2 * (1 - lax.rem(lax.div(lax.axis_index("col"), 2), 2))
    dims = (((1,), (0,)), ((), ()))
    for side, panel in ((0, own), (1, other)):
        total = jnp.zeros((ROWS * HALF, WIDTH), jnp.float32)
        for part in range(4):
            q, half = divmod(part, 2)
            left = jnp.concatenate(
                [
                    square[(2 * i + (q ^ high)) ^ turn, :, half * WIDTH : (half + 1) * WIDTH]
                    for i in range(ROWS)
                ],
                axis=0,
            )
            total += triple_dot(left, panel_part(panel, panel_kept, side, part), dims)
        for i in range(ROWS):
            out[lax.rem(i + first, ROWS), lax.rem(core + side, 2)] = total[i * HALF : (i + 1) * HALF]


def finish_kernel(cube, mirrored, square, purified):
    home = mirrored[...].T
    square[...] = home
    for c in range(2):
        rows = slice(c * HALF, (c + 1) * HALF)
        total = (cube[c] + cube[2 + c]) + (cube[4 + c] + cube[6 + c])
        purified[rows] = 3.0 * home[rows] - 2.0 * total


def call(kernel, shapes, *operands, flops):
    return pl.pallas_call(
        kernel,
        out_shape=[jax.ShapeDtypeStruct(shape, jnp.float32) for shape in shapes],
        in_specs=[pl.BlockSpec(memory_space=pltpu.VMEM)] * len(operands),
        out_specs=[pl.BlockSpec(memory_space=pltpu.VMEM)] * len(shapes),
        compiler_params=pltpu.CompilerParams(vmem_limit_bytes=32 * 1024 * 1024),
        cost_estimate=pl.CostEstimate(
            flops=flops, bytes_accessed=1024 * 1024, transcendentals=0
        ),
    )(*operands)


def kept_columns(pattern, col):
    both = [lax.dynamic_slice_in_dim(pattern, 2 * (col ^ side), 2, axis=1) for side in range(2)]
    return jnp.repeat(jnp.stack(both).astype(jnp.float32), BLK, axis=2)


def swap_core(value):
    return lax.ppermute(value, "col", [(i, i ^ 1) for i in range(16)])


def near_exchange(value):
    groups = [[(chip ^ 4 * core) * 2 + core for chip in range(NEAR)] for core in range(2)]
    return lax.all_to_all(value, "col", 0, 0, axis_index_groups=groups)


def copies(value, count):
    return jnp.broadcast_to(value[None], (count, *value.shape))


def mirror_home(piece):
    pairs = []
    for r in range(4):
        for c in range(16):
            for z in range(LAYERS):
                to = (r * 16 + c // 4 * 4 + z // 2) * LAYERS + (z ^ (2 * (c % 4)))
                pairs.append(((r * 16 + c) * LAYERS + z, to))
    return lax.ppermute(piece, ("row", "col", "layer"), pairs)


def layer_pair(pieces, layer):
    received = lax.ppermute(pieces[1], "layer", [(z, z ^ 1) for z in range(LAYERS)])
    return jnp.where(
        layer % 2 == 0,
        jnp.concatenate([pieces[0], received], axis=0),
        jnp.concatenate([received, pieces[0]], axis=0),
    )


def whole_rows(piece, core, layer):
    blocks = [piece[:, k * BLK : (k + 1) * BLK] for k in range(4)]
    blocks = jnp.stack(blocks)
    pick = lambda c: jnp.stack(
        [
            lax.dynamic_index_in_dim(blocks, (layer % 4) ^ (2 * c + j), 0, keepdims=False)
            for j in range(2)
        ]
    )
    mine, theirs = pick(core), swap_core(pick(1 - core))
    return jnp.where(
        core == 0,
        jnp.concatenate([mine, theirs], axis=1),
        jnp.concatenate([theirs, mine], axis=1),
    )


def body(density, pattern):
    row, col, layer = (lax.axis_index(name) for name in ("row", "col", "layer"))
    core = col % 2
    row_groups = pattern.reshape(ROWS, LAYERS, ROWS * LAYERS)
    panel_kept = kept_columns(lax.dynamic_index_in_dim(row_groups, row, 0, keepdims=False), col)
    rows_kept = kept_columns(lax.dynamic_index_in_dim(row_groups, layer, 1, keepdims=False), col)

    lines = [[c * LAYERS + (z ^ 4 * (1 - c % 2)) for z in range(LAYERS)] for c in range(16)]
    own = lax.all_to_all(
        copies(density, LAYERS), ("col", "layer"), 0, 0, axis_index_groups=lines
    ).reshape(LAYERS * BLK, WIDTH)

    halves = density.reshape(2, HALF, WIDTH)
    mine = lax.dynamic_index_in_dim(halves, core, 0, keepdims=False)
    theirs = lax.dynamic_index_in_dim(halves, 1 - core, 0, keepdims=False)
    rows = jnp.concatenate([mine, swap_core(theirs)], axis=0)
    rows = lax.all_gather(rows, "row").reshape(ROWS, 2, HALF, WIDTH)

    own, rows = lax.optimization_barrier((own, rows))
    other = swap_core(own)
    flops = 6 * 256 * 512 * 1024
    (square_terms,) = call(
        first_kernel,
        [(NEAR, HALF, 2 * WIDTH)],
        rows,
        own,
        other,
        rows_kept,
        panel_kept,
        flops=flops,
    )
    square_piece = jnp.sum(near_exchange(square_terms), axis=0)
    square_rows = near_exchange(copies(square_piece, NEAR))
    piece = layer_pair(whole_rows(square_piece, core, layer), layer)
    square_rows, piece = lax.optimization_barrier((square_rows, piece))
    mirrored = mirror_home(piece)

    (cube_terms,) = call(
        second_kernel,
        [(ROWS, 2, HALF, WIDTH)],
        square_rows,
        own,
        other,
        panel_kept,
        flops=flops,
    )
    homes = [
        [(r + 2 * (1 - chip % 2)) % ROWS * 16 + chip * 2 + c for r in range(ROWS) for c in range(2)]
        for chip in range(NEAR)
    ]
    cube_terms = cube_terms.reshape(ROWS * 2, HALF, WIDTH)
    cube = lax.all_to_all(cube_terms, ("row", "col"), 0, 0, axis_index_groups=homes)
    cube, mirrored = lax.optimization_barrier((cube, mirrored))
    square, purified = call(
        finish_kernel, [(BLK, WIDTH)] * 2, cube, mirrored, flops=16 * BLK * WIDTH
    )
    return (square, purified)


def solution(mesh):
    in_specs = (P(("row", "layer"), "col"), P())
    out_specs = (P(("row", "layer"), "col"), P(("row", "layer"), "col"))
    return jax.shard_map(body, mesh=mesh, in_specs=in_specs, out_specs=out_specs, check_vma=False)
```
